768 devices in a mesh: group: 96 (over z, y), local: 8 (over x, core).
Axes of the slice: x: 4, y: 8, z: 12, core: 2. Of those that a mesh axis runs over, the one named last changes fastest.
Arguments:
- features: bfloat16 [786432, 256], P(('group', 'local')), may hold values from -6 to 6
- aggregate: bfloat16 [786432, 256], P(('group', 'local')), may hold values from -6 to 6
- preact: bfloat16 [786432, 256], P(('group', 'local')), may hold values from -8 to 8
- cotangent: bfloat16 [786432, 256], P(('group', 'local')), may hold values from -6 to 6
- w_self: bfloat16 [256, 256], replicated, may hold values from -0.375 to 0.375
- w_neigh: bfloat16 [256, 256], replicated, may hold values from -0.375 to 0.375
- tile_vals: bfloat16 [49152, 128, 128], P(('group', 'local')), may hold values from -0.1875 to 0.1875
- tile_rows: int32 [49152], P(('group', 'local')), may hold values from 0 to 7
- tile_cols: int32 [49152], P(('group', 'local')), may hold values from 0 to 7
- edge_dst: int32 [1572864], P(('group', 'local')), may hold values from 0 to 1023
- edge_slot: int32 [1572864], P(('group', 'local')), may hold values from 0 to 1535
- edge_weight: float32 [1572864], P(('group', 'local')), may hold values from 0.1 to 1
- recv_rows: int32 [96, 96, 16], P('group', None, 'local'), may hold values from 0 to 1023
Outputs:
- grad_x: bfloat16 [786432, 256], P(('group', 'local'))
- grad_self_w: float32 [256, 256], replicated
- grad_neigh_w: float32 [256, 256], replicated
The draws below stay inside these ranges and needn't reach their ends.
All inputs are finite; a program needn't handle non-finite values.
Results may differ from the reference program's by a relative error of at most 0.014.
Values may be sent and summed in bfloat16 or wider, within the bound.
No kernel may reach another device: no remote copies, remote signals or barrier semaphores. Data moves between devices by JAX's collectives and lax.ppermute only.
A program may use at most 64 MiB of HBM per device.

```python
import math
import jax
import jax.numpy as jnp
import numpy as np
from jax import lax

H = 256
BLK = 128
NBLK = 8
TI = 64
EB = 2048
BR_OWN = 2
NODE_DEV = 1024
NODES = 786432
BR = 16
N_GROUP = 96
N_LOCAL = 8
DEVICES = 768


def plant(result, rng, smallest, high):
    shape = result.shape
    index_at = [jax.random.randint(jax.random.fold_in(rng, axis), (), 0, shape[axis]) for axis in range(len(shape))]
    result = result.at[tuple(index_at)].set(smallest)
    longest = shape.index(max(shape))
    index_at[longest] = (index_at[longest] + 1) % shape[longest]
    return result.at[tuple(index_at)].set(high)


def steps_of(own_key, shape, shards, low, largest):
    def one(dim, blocks):
        draws = jax.random.uniform(jax.random.fold_in(jax.random.fold_in(own_key, 6), dim), (blocks,), jnp.float32, low / len(shards), largest / len(shards))
        return jnp.repeat(jnp.exp(draws), shape[dim] // blocks).reshape((-1,) + (1,) * (len(shape) - dim - 1))

    gain = one(*shards[0])
    for cut in shards[1:]:
        gain = gain * one(*cut)
    return gain


def rank_bounds(amount, slope):
    portions = [(1 << 20) // math.isqrt(grade ** slope) + 1 for grade in range(1, amount + 1)]
    deviation = 1 + sum(portions) // (1 << 30)
    return np.cumsum(np.array([max(1, weight // deviation) for weight in portions]))


def ranked_ids(stream_key, dims, amount, skew):
    grid = rank_bounds(amount, skew)
    pick = jax.random.randint(jax.random.fold_in(stream_key, 1), dims, 0, int(grid[amount - 1]))
    grade = jnp.searchsorted(jnp.asarray(grid, jnp.int32), pick, side="right")
    return jax.random.permutation(jax.random.fold_in(stream_key, 2), amount)[grade].astype(jnp.int32)


def scatter_about(rng, extent, width, bound, split=(), held_as=jnp.bfloat16):
    values = width * jax.random.normal(rng, extent, jnp.float32)
    if split:
        values = values * steps_of(rng, extent, split, -0.22, 0.18)
    return jnp.clip(values, -bound, bound).astype(held_as)


def setup_inputs(seed: int = 0) -> dict:
    splits = jax.random.split(jax.random.key(seed), 14)
    return {
        "features": scatter_about(splits[0], (NODES, H), 1.0, 6.0, ((0, 768),)),
        "aggregate": scatter_about(splits[1], (NODES, H), 1.0, 6.0, ((0, 768),)),
        "preact": scatter_about(splits[2], (NODES, H), 1.5, 8.0, ((0, 768),)),
        "cotangent": scatter_about(splits[3], (NODES, H), 1.0, 6.0, ((0, 768),)),
        "w_self": scatter_about(splits[4], (H, H), H ** -0.5, 0.375),
        "w_neigh": scatter_about(splits[5], (H, H), H ** -0.5, 0.375),
        "tile_vals": scatter_about(splits[6], (TI * DEVICES, BLK, BLK), (BLK * TI // NBLK) ** -0.5, 0.1875, ((0, 768),)),
        "tile_rows": plant(jax.random.randint(splits[7], (TI * DEVICES,), 0, NBLK), jax.random.fold_in(splits[7], 1), 0, NBLK - 1).astype(jnp.int32),
        "tile_cols": plant(jax.random.randint(splits[8], (TI * DEVICES,), 0, NBLK), jax.random.fold_in(splits[8], 1), 0, NBLK - 1).astype(jnp.int32),
        "edge_dst": plant(jax.random.randint(splits[9], (EB * DEVICES,), 0, NODE_DEV), jax.random.fold_in(splits[9], 1), 0, NODE_DEV - 1).astype(jnp.int32),
        "edge_slot": plant(ranked_ids(splits[10], (EB * DEVICES,), N_GROUP * BR, 1), jax.random.fold_in(splits[10], 3), 0, (N_GROUP * BR) - 1).astype(jnp.int32),
        "edge_weight": jnp.clip(0.1 + 0.9 * jax.random.uniform(splits[11], (EB * DEVICES,), jnp.float32) ** steps_of(splits[11], (EB * DEVICES,), ((0, 768),), -0.2, 0.2), 0.1, 1.0),
        "recv_rows": plant(jax.random.randint(splits[12], (N_GROUP, N_GROUP, BR), 0, NODE_DEV), jax.random.fold_in(splits[12], 1), 0, NODE_DEV - 1).astype(jnp.int32),
    }


def rows_product(first_op, second_op):
    return lax.dot_general(first_op, second_op, (((0,), (0,)), ((), ())), preferred_element_type=jnp.float32)

def times_transposed(first_op, second_op):
    return lax.dot_general(first_op, second_op, (((1,), (1,)), ((), ())), preferred_element_type=jnp.float32)

def reference(features, aggregate, preact, cotangent, w_self, w_neigh, tile_vals, tile_rows, tile_cols, edge_dst, edge_slot, edge_weight, recv_rows):
    devices_count = N_GROUP * N_LOCAL
    grad_scale = NODES ** (-0.5)
    preact_f = preact.astype(jnp.float32)
    gate_sig = jax.nn.sigmoid(preact_f)
    d_preact = (cotangent.astype(jnp.float32) * gate_sig * (1.0 + preact_f * (1.0 - gate_sig))).astype(jnp.bfloat16)
    grad_self_w = rows_product(features, d_preact) * grad_scale
    grad_neigh_w = rows_product(aggregate, d_preact) * grad_scale
    pushed = times_transposed(d_preact, w_neigh).astype(jnp.bfloat16)
    pushed_groups = pushed.reshape(N_GROUP, N_LOCAL * NODE_DEV, H)
    member_base = (jnp.arange(N_LOCAL, dtype=jnp.int32) * NODE_DEV)[:, None]
    dst_groups = (edge_dst.reshape(N_GROUP, N_LOCAL, EB).astype(jnp.int32) + member_base).reshape(N_GROUP, N_LOCAL * EB)
    slot_groups = edge_slot.reshape(N_GROUP, N_LOCAL * EB)
    weight_groups = edge_weight.reshape(N_GROUP, N_LOCAL * EB)

    def group_partial(items):
        rows_here, dst_here, slot_here, weight_here = items
        edge_terms = jnp.take(rows_here, dst_here, axis=0).astype(jnp.float32) * weight_here[:, None]
        summed = jax.ops.segment_sum(edge_terms, slot_here, num_segments=N_GROUP * BR)
        return summed.astype(jnp.bfloat16)
    group_sum = lax.map(group_partial, (pushed_groups, dst_groups, slot_groups, weight_groups))
    arriving = group_sum.reshape(N_GROUP, N_GROUP, N_LOCAL, BR_OWN, H).transpose(1, 2, 0, 3, 4)
    arriving = arriving.reshape(devices_count, N_GROUP * BR_OWN, H)
    targets = recv_rows.reshape(N_GROUP, N_GROUP, N_LOCAL, BR_OWN).transpose(0, 2, 1, 3)
    targets = targets.reshape(devices_count, N_GROUP * BR_OWN)

    def device_grad(items):
        dpre_here, pushed_here, vals_here, rows_idx, cols_idx, arrived_here, target_here = items
        own_term = times_transposed(dpre_here, w_self)
        src_blocks = jnp.take(pushed_here.reshape(NBLK, BLK, H), rows_idx, axis=0)
        contrib = jnp.einsum('tij,tih->tjh', vals_here.astype(jnp.float32), src_blocks.astype(jnp.float32))
        interior = jax.ops.segment_sum(contrib, cols_idx, num_segments=NBLK).reshape(NODE_DEV, H)
        incoming = jax.ops.segment_sum(arrived_here.astype(jnp.float32), target_here, num_segments=NODE_DEV)
        return (own_term + interior + incoming).astype(jnp.bfloat16)
    grad_x = lax.map(device_grad, (d_preact.reshape(devices_count, NODE_DEV, H), pushed.reshape(devices_count, NODE_DEV, H), tile_vals.reshape(devices_count, TI, BLK, BLK), tile_rows.reshape(devices_count, TI), tile_cols.reshape(devices_count, TI), arriving, targets))
    return (grad_x.reshape(NODES, H), grad_self_w, grad_neigh_w)
```

```python
import jax
import jax.numpy as jnp
from jax import lax
from jax.experimental import pallas as pl
from jax.experimental.pallas import tpu as pltpu
from jax.sharding import PartitionSpec as P

F32 = jnp.float32
BF16 = jnp.bfloat16
VMEM_LIMIT = 48 * 1024 * 1024


def dot_nn(first_op, second_op):
    return lax.dot_general(first_op, second_op, (((1,), (0,)), ((), ())), preferred_element_type=F32)


def dot_nt(first_op, second_op):
    return lax.dot_general(first_op, second_op, (((1,), (1,)), ((), ())), preferred_element_type=F32)


def identity(size):
    row = lax.broadcasted_iota(jnp.int32, (size, size), 0)
    col = lax.broadcasted_iota(jnp.int32, (size, size), 1)
    return jnp.where(row == col, 1.0, 0.0).astype(BF16)


def edges_and_grads(groups, members, per_owner, scale, chunk):
    def kernel(
        preact_ref, cot_ref, feat_ref, agg_ref, wn_ref, dst_ref, slot_ref, weight_ref, dp_ref, pushed_ref, part_ref
    ):
        nodes, width = preact_ref.shape
        edges = dst_ref.shape[1]
        x = preact_ref[...].astype(F32)
        sig = jax.nn.sigmoid(x)
        dp = (cot_ref[...].astype(F32) * sig * (1.0 + x * (1.0 - sig))).astype(BF16)
        dp_ref[...] = dp
        pushed_t = dot_nt(wn_ref[...], dp).astype(BF16)
        pushed_ref[...] = pushed_t

        eye = identity(width)
        rows_per_member = 2 * width // members
        per_grad = width // rows_per_member
        for which, ref in enumerate((feat_ref, agg_ref)):
            ref_t = dot_nt(eye, ref[...]).astype(BF16)
            grad = (dot_nn(ref_t, dp) * scale).astype(BF16)
            for k in range(per_grad):
                m = which * per_grad + k
                part_ref[m, 0:rows_per_member, per_owner * width :] = grad[
                    k * rows_per_member : (k + 1) * rows_per_member
                ]
                part_ref[m, rows_per_member:, per_owner * width :] = jnp.zeros(
                    (groups - rows_per_member, width), BF16
                )

        rows = members * groups
        for e0 in range(0, edges, chunk):
            dst = dst_ref[:, e0 : e0 + chunk]
            node = lax.broadcasted_iota(jnp.int32, (nodes, chunk), 0)
            take = jnp.where(node == dst, 1.0, 0.0).astype(BF16)
            terms = (dot_nn(pushed_t, take) * weight_ref[:, e0 : e0 + chunk]).astype(BF16)
            terms_ref_value = terms
            if e0 == 0:
                all_terms = [terms_ref_value]
            else:
                all_terms.append(terms_ref_value)
        terms = jnp.concatenate(all_terms, axis=1)

        slot = slot_ref[...]
        per_group = members * per_owner
        group = slot // per_group
        rest = slot - group * per_group
        member = rest // per_owner
        which = rest - member * per_owner
        place = which * rows + member * groups + group
        for j in range(per_owner):
            for m in range(members):
                base = j * rows + m * groups
                row = lax.broadcasted_iota(jnp.int32, (groups, edges), 0) + base
                put = jnp.where(row == place, 1.0, 0.0).astype(BF16)
                part_ref[m, :, j * width : (j + 1) * width] = dot_nt(put, terms).astype(BF16)

    return kernel


def tiles_kernel(rows_ref, cols_ref, vals_ref, pushed_ref, dp_ref, ws_ref, out_ref, adj_ref):
    count, block, _ = vals_ref.shape
    adj_ref[...] = jnp.zeros_like(adj_ref)

    def add(t, carry):
        at = (pl.ds(rows_ref[t] * block, block), pl.ds(pl.multiple_of(cols_ref[t] * block, block), block))
        adj_ref[at] += vals_ref[t].astype(F32)
        return carry

    lax.fori_loop(0, count, add, 0)
    interior_t = dot_nn(pushed_ref[...], adj_ref[...].astype(BF16))
    out_ref[...] = dot_nt(dp_ref[...], ws_ref[...]) + interior_t.T


def finish_kernel(arrived_ref, target_ref, base_ref, out_ref, row_ref):
    nodes, width = out_ref.shape
    groups = arrived_ref.shape[0]
    per_owner = target_ref.shape[0]
    arrived = arrived_ref[...]
    total = base_ref[...]
    for j in range(per_owner):
        node = lax.broadcasted_iota(jnp.int32, (nodes, groups), 0)
        put = jnp.where(node == target_ref[j : j + 1, :], 1.0, 0.0).astype(BF16)
        total += dot_nn(put, arrived[:, j * width : (j + 1) * width])
    out_ref[...] = total.astype(BF16)
    row_ref[...] = jnp.sum(
        arrived[:, per_owner * width :].astype(F32), axis=0, keepdims=True
    ).astype(BF16)


def on_device(
    features,
    aggregate,
    preact,
    cotangent,
    w_self,
    w_neigh,
    tile_vals,
    tile_rows,
    tile_cols,
    edge_dst,
    edge_slot,
    edge_weight,
    recv_rows,
):
    groups = lax.axis_size("group")
    members = lax.axis_size("local")
    nodes, width = features.shape
    edges = edge_dst.shape[0]
    per_owner = recv_rows.shape[2]
    scale = (nodes * groups * members) ** (-0.5)
    payload = (per_owner + 1) * width
    share = 2 * width // members
    params = pltpu.CompilerParams(vmem_limit_bytes=VMEM_LIMIT)

    dp, pushed_t, part = pl.pallas_call(
        edges_and_grads(groups, members, per_owner, scale, 512),
        out_shape=(
            jax.ShapeDtypeStruct((nodes, width), BF16),
            jax.ShapeDtypeStruct((width, nodes), BF16),
            jax.ShapeDtypeStruct((members, groups, payload), BF16),
        ),
        compiler_params=params,
        name="edges_and_grads",
    )(
        preact,
        cotangent,
        features,
        aggregate,
        w_neigh,
        edge_dst.reshape(1, edges),
        edge_slot.reshape(1, edges),
        edge_weight.reshape(1, edges),
    )
    smem = pl.BlockSpec(memory_space=pltpu.SMEM)
    vmem = pl.BlockSpec(memory_space=pltpu.VMEM)
    base = pl.pallas_call(
        tiles_kernel,
        out_shape=jax.ShapeDtypeStruct((nodes, width), F32),
        in_specs=[smem, smem, vmem, vmem, vmem, vmem],
        scratch_shapes=[pltpu.VMEM((nodes, nodes), F32)],
        compiler_params=params,
        name="tiles",
    )(tile_rows, tile_cols, tile_vals, pushed_t, dp, w_self)

    part = lax.all_to_all(part, "local", 0, 0, tiled=True)
    summed = part.astype(F32).sum(0).astype(BF16)
    arrived = lax.all_to_all(summed, "group", 0, 0, tiled=True)
    grad_x, row = pl.pallas_call(
        finish_kernel,
        out_shape=(
            jax.ShapeDtypeStruct((nodes, width), BF16),
            jax.ShapeDtypeStruct((1, width), BF16),
        ),
        compiler_params=params,
        name="finish",
    )(arrived, recv_rows.reshape(groups, per_owner).T, base)
    spread = lax.all_to_all(jnp.broadcast_to(row, (groups, width)), "group", 0, 0, tiled=True)
    mine = spread[:share]
    grads = lax.all_to_all(jnp.broadcast_to(mine[None], (members, share, width)), "local", 0, 0, tiled=True)
    grads = grads.reshape(2, width, width).astype(F32)
    return (grad_x, grads[0], grads[1])


def solution(mesh):
    both = ("group", "local")
    placed = (
        P(both, None),
        P(both, None),
        P(both, None),
        P(both, None),
        P(),
        P(),
        P(both, None, None),
        P(both),
        P(both),
        P(both),
        P(both),
        P(both),
        P("group", None, "local"),
    )
    return jax.shard_map(
        on_device,
        mesh=mesh,
        in_specs=placed,
        out_specs=(P(both, None), P(), P()),
        check_vma=False,
    )
```

```python
import jax
import jax.numpy as jnp
from jax import lax
from jax.experimental import pallas as pl
from jax.experimental.pallas import tpu as pltpu
from jax.sharding import PartitionSpec as P

F32 = jnp.float32
BF16 = jnp.bfloat16
VMEM_LIMIT = 24 * 1024 * 1024


def dot_nn(first_op, second_op):
    return lax.dot_general(first_op, second_op, (((1,), (0,)), ((), ())), preferred_element_type=F32)


def dot_nt(first_op, second_op):
    return lax.dot_general(first_op, second_op, (((1,), (1,)), ((), ())), preferred_element_type=F32)


def identity(size):
    row = lax.broadcasted_iota(jnp.int32, (size, size), 0)
    col = lax.broadcasted_iota(jnp.int32, (size, size), 1)
    return jnp.where(row == col, 1.0, 0.0).astype(BF16)


def edges_and_grads(groups, members, per_owner, scale, chunk):
    def kernel(
        preact_hbm, cot_hbm, wn_hbm, dst_hbm, slot_hbm, weight_hbm, feat_hbm, agg_hbm,
        dp_hbm, pushed_hbm, send_ref, keep_ref,
        preact_ref, cot_ref, wn_ref, dst_ref, slot_ref, weight_ref, feat_ref, agg_ref,
        dp_ref, pushed_ref, in_sem, out_sem,
    ):
        sources = (preact_hbm, cot_hbm, wn_hbm, dst_hbm, slot_hbm, weight_hbm, feat_hbm, agg_hbm)
        held = (preact_ref, cot_ref, wn_ref, dst_ref, slot_ref, weight_ref, feat_ref, agg_ref)
        loads = [pltpu.make_async_copy(s, d, in_sem.at[i]) for i, (s, d) in enumerate(zip(sources, held))]
        for load in loads:
            load.start()
        nodes, width = preact_ref.shape
        edges = dst_ref.shape[1]
        side = lax.rem(lax.axis_index("local"), 2)
        for load in loads[:6]:
            load.wait()
        x = preact_ref[...].astype(F32)
        sig = jax.nn.sigmoid(x)
        dp = (cot_ref[...].astype(F32) * sig * (1.0 + x * (1.0 - sig))).astype(BF16)
        dp_ref[...] = dp
        pushed_t = dot_nt(wn_ref[...], dp).astype(BF16)
        pushed_ref[...] = pushed_t
        stores = [
            pltpu.make_async_copy(dp_ref, dp_hbm, out_sem.at[0]),
            pltpu.make_async_copy(pushed_ref, pushed_hbm, out_sem.at[1]),
        ]
        for store in stores:
            store.start()

        all_terms = []
        for e0 in range(0, edges, chunk):
            dst = dst_ref[:, e0 : e0 + chunk]
            node = lax.broadcasted_iota(jnp.int32, (nodes, chunk), 0)
            take = jnp.where(node == dst, 1.0, 0.0).astype(BF16)
            all_terms.append((dot_nn(pushed_t, take) * weight_ref[:, e0 : e0 + chunk]).astype(BF16))
        terms = jnp.concatenate(all_terms, axis=1)

        slot = slot_ref[...]
        per_group = members * per_owner
        rows = members * groups
        group = slot // per_group
        rest = slot - group * per_group
        member = rest // per_owner
        which = rest - member * per_owner
        place = which * rows + member * groups + group
        for ref, parity in ((send_ref, 1 - side), (keep_ref, side)):
            for j in range(per_owner):
                for p in range(members // 2):
                    base = j * rows + (2 * p + parity) * groups
                    row = lax.broadcasted_iota(jnp.int32, (groups, edges), 0)
                    put = jnp.where(row == place - base, 1.0, 0.0).astype(BF16)
                    ref[p, :, j * width : (j + 1) * width] = dot_nt(put, terms).astype(BF16)

        for load in loads[6:]:
            load.wait()
        eye = identity(width)
        share = 2 * width // members
        empty = jnp.zeros((groups - share, width), BF16)
        lanes = slice(per_owner * width, (per_owner + 1) * width)
        for i, ref in enumerate((feat_ref, agg_ref)):
            grad = dot_nn(dot_nt(eye, ref[...]).astype(BF16), dp) * scale
            for k in range(members // 4):
                p = i * (members // 4) + k
                low = grad[2 * k * share : (2 * k + 1) * share]
                high = grad[(2 * k + 1) * share : (2 * k + 2) * share]
                send_ref[p, 0:share, lanes] = jnp.where(side == 0, high, low).astype(BF16)
                keep_ref[p, 0:share, lanes] = jnp.where(side == 0, low, high).astype(BF16)
                send_ref[p, share:, lanes] = empty
                keep_ref[p, share:, lanes] = empty
        for store in stores:
            store.wait()

    return kernel


def tiles_kernel(rows_ref, cols_ref, vals_ref, pushed_ref, dp_ref, ws_ref, out_ref, adj_ref):
    count, block, _ = vals_ref.shape
    adj_ref[...] = jnp.zeros_like(adj_ref)

    def add(t, carry):
        rows = pl.ds(pl.multiple_of(rows_ref[t] * block, block), block)
        cols = pl.ds(pl.multiple_of(cols_ref[t] * block, block), block)
        adj_ref[rows, cols] += vals_ref[t].astype(F32)
        return carry

    lax.fori_loop(0, count, add, 0)
    interior_t = dot_nn(pushed_ref[...], adj_ref[...].astype(BF16))
    out_ref[...] = dot_nt(dp_ref[...], ws_ref[...]) + interior_t.T


def finish_kernel(arrived_ref, target_ref, base_ref, out_ref):
    nodes, width = out_ref.shape
    groups = arrived_ref.shape[0]
    per_owner = target_ref.shape[0]
    arrived = arrived_ref[...]
    total = base_ref[...]
    for j in range(per_owner):
        node = lax.broadcasted_iota(jnp.int32, (nodes, groups), 0)
        put = jnp.where(node == target_ref[j : j + 1, :], 1.0, 0.0).astype(BF16)
        total += dot_nn(put, arrived[:, j * width : (j + 1) * width])
    out_ref[...] = total.astype(BF16)


def on_device(
    features,
    aggregate,
    preact,
    cotangent,
    w_self,
    w_neigh,
    tile_vals,
    tile_rows,
    tile_cols,
    edge_dst,
    edge_slot,
    edge_weight,
    recv_rows,
):
    groups = lax.axis_size("group")
    members = lax.axis_size("local")
    nodes, width = features.shape
    edges = edge_dst.shape[0]
    per_owner = recv_rows.shape[2]
    scale = (nodes * groups * members) ** (-0.5)
    payload = (per_owner + 1) * width
    share = 2 * width // members
    params = pltpu.CompilerParams(vmem_limit_bytes=VMEM_LIMIT)
    smem = pl.BlockSpec(memory_space=pltpu.SMEM)
    vmem = pl.BlockSpec(memory_space=pltpu.VMEM)
    hbm = pl.BlockSpec(memory_space=pltpu.HBM)

    operands = (
        preact,
        cotangent,
        w_neigh,
        edge_dst.reshape(1, edges),
        edge_slot.reshape(1, edges),
        edge_weight.reshape(1, edges),
        features,
        aggregate,
    )
    half = jax.ShapeDtypeStruct((members // 2, groups, payload), BF16)
    dp, pushed_t, send, keep = pl.pallas_call(
        edges_and_grads(groups, members, per_owner, scale, 512),
        out_shape=(
            jax.ShapeDtypeStruct((nodes, width), BF16),
            jax.ShapeDtypeStruct((width, nodes), BF16),
            half,
            half,
        ),
        in_specs=[hbm] * len(operands),
        out_specs=(hbm, hbm, vmem, vmem),
        scratch_shapes=[pltpu.VMEM(a.shape, a.dtype) for a in operands]
        + [
            pltpu.VMEM((nodes, width), BF16),
            pltpu.VMEM((width, nodes), BF16),
            pltpu.SemaphoreType.DMA((len(operands),)),
            pltpu.SemaphoreType.DMA((2,)),
        ],
        compiler_params=params,
        name="edges_and_grads",
    )(*[pltpu.with_memory_space_constraint(a, pltpu.HBM) for a in operands])
    base = pl.pallas_call(
        tiles_kernel,
        out_shape=jax.ShapeDtypeStruct((nodes, width), F32),
        in_specs=[smem, smem, vmem, vmem, vmem, vmem],
        out_specs=vmem,
        scratch_shapes=[pltpu.VMEM((nodes, nodes), F32)],
        compiler_params=params,
        name="tiles",
    )(tile_rows, tile_cols, tile_vals, pushed_t, dp, w_self)

    other_core = [(i, i ^ 1) for i in range(members)]
    along_x = [list(range(core, members, 2)) for core in range(2)]
    came = lax.ppermute(send, "local", other_core)
    chip_sum = (came.astype(F32) + keep.astype(F32)).astype(BF16)
    parts = lax.all_to_all(chip_sum, "local", 0, 0, axis_index_groups=along_x, tiled=True)
    summed = parts.astype(F32).sum(0).astype(BF16)
    arrived = lax.all_to_all(summed, "group", 0, 0, tiled=True)
    row = arrived[:, per_owner * width :].astype(F32).sum(0, keepdims=True).astype(BF16)
    spread = lax.all_to_all(jnp.broadcast_to(row, (groups, width)), "group", 0, 0, tiled=True)
    grad_x = pl.pallas_call(
        finish_kernel,
        out_shape=jax.ShapeDtypeStruct((nodes, width), BF16),
        compiler_params=params,
        name="finish",
    )(arrived, recv_rows.reshape(groups, per_owner).T, base)
    mine = spread[:share]
    grads = lax.all_to_all(jnp.broadcast_to(mine[None], (members, share, width)), "local", 0, 0, tiled=True)
    grads = grads.reshape(2, width, width).astype(F32)
    return (grad_x, grads[0], grads[1])


def solution(mesh):
    both = ("group", "local")
    placed = (
        P(both, None),
        P(both, None),
        P(both, None),
        P(both, None),
        P(),
        P(),
        P(both, None, None),
        P(both),
        P(both),
        P(both),
        P(both),
        P(both),
        P("group", None, "local"),
    )
    return jax.shard_map(
        on_device,
        mesh=mesh,
        in_specs=placed,
        out_specs=(P(both, None), P(), P()),
        check_vma=False,
    )
```

```python
import jax
import jax.numpy as jnp
from jax import lax
from jax.experimental import pallas as pl
from jax.experimental.pallas import tpu as pltpu
from jax.sharding import PartitionSpec as P

F32 = jnp.float32
BF16 = jnp.bfloat16
VMEM_LIMIT = 24 * 1024 * 1024


def dot_nn(first_op, second_op):
    return lax.dot_general(first_op, second_op, (((1,), (0,)), ((), ())), preferred_element_type=F32)


def dot_nt(first_op, second_op):
    return lax.dot_general(first_op, second_op, (((1,), (1,)), ((), ())), preferred_element_type=F32)


def identity(size):
    row = lax.broadcasted_iota(jnp.int32, (size, size), 0)
    col = lax.broadcasted_iota(jnp.int32, (size, size), 1)
    return jnp.where(row == col, 1.0, 0.0).astype(BF16)


def edges_and_grads(groups, members, per_owner, scale, chunk):
    def kernel(
        dst_hbm, slot_hbm, weight_hbm, preact_hbm, cot_hbm, wn_hbm, feat_hbm, agg_hbm,
        dp_hbm, pushed_hbm, send_ref, keep_ref,
        dst_ref, slot_ref, weight_ref, preact_ref, cot_ref, wn_ref, feat_ref, agg_ref,
        dp_ref, pushed_ref, put_ref, in_sem, out_sem,
    ):
        sources = (dst_hbm, slot_hbm, weight_hbm, preact_hbm, cot_hbm, wn_hbm, feat_hbm, agg_hbm)
        held = (dst_ref, slot_ref, weight_ref, preact_ref, cot_ref, wn_ref, feat_ref, agg_ref)
        loads = [pltpu.make_async_copy(s, d, in_sem.at[i]) for i, (s, d) in enumerate(zip(sources, held))]
        for load in loads:
            load.start()
        nodes, width = preact_ref.shape
        edges = dst_ref.shape[1]
        side = lax.rem(lax.axis_index("local"), 2)
        for load in loads[:3]:
            load.wait()
        slot = slot_ref[...]
        per_group = members * per_owner
        rows = members * groups
        group = slot // per_group
        rest = slot - group * per_group
        member = rest // per_owner
        which = rest - member * per_owner
        place = which * rows + member * groups + group
        row = lax.broadcasted_iota(jnp.int32, (groups, edges), 0)
        pieces = [
            (ref, j, p, j * rows + (2 * p + parity) * groups)
            for ref, parity in ((send_ref, 1 - side), (keep_ref, side))
            for j in range(per_owner)
            for p in range(members // 2)
        ]
        for n, (_, _, _, first) in enumerate(pieces):
            put_ref[n] = jnp.where(row == place - first, 1.0, 0.0).astype(BF16)
        for load in loads[3:6]:
            load.wait()
        x = preact_ref[...].astype(F32)
        sig = jax.nn.sigmoid(x)
        dp = (cot_ref[...].astype(F32) * sig * (1.0 + x * (1.0 - sig))).astype(BF16)
        dp_ref[...] = dp
        pushed_t = dot_nt(wn_ref[...], dp).astype(BF16)
        pushed_ref[...] = pushed_t
        stores = [
            pltpu.make_async_copy(dp_ref, dp_hbm, out_sem.at[0]),
            pltpu.make_async_copy(pushed_ref, pushed_hbm, out_sem.at[1]),
        ]
        for store in stores:
            store.start()

        all_terms = []
        for e0 in range(0, edges, chunk):
            dst = dst_ref[:, e0 : e0 + chunk]
            node = lax.broadcasted_iota(jnp.int32, (nodes, chunk), 0)
            take = jnp.where(node == dst, 1.0, 0.0).astype(BF16)
            all_terms.append((dot_nn(pushed_t, take) * weight_ref[:, e0 : e0 + chunk]).astype(BF16))
        terms = jnp.concatenate(all_terms, axis=1)

        for n, (ref, j, p, _) in enumerate(pieces):
            ref[p, :, j * width : (j + 1) * width] = dot_nt(put_ref[n], terms).astype(BF16)

        for load in loads[6:]:
            load.wait()
        eye = identity(width)
        share = 2 * width // members
        empty = jnp.zeros((groups - share, width), BF16)
        lanes = slice(per_owner * width, (per_owner + 1) * width)
        for i, ref in enumerate((feat_ref, agg_ref)):
            grad = dot_nn(dot_nt(eye, ref[...]).astype(BF16), dp) * scale
            for k in range(members // 4):
                p = i * (members // 4) + k
                low = grad[2 * k * share : (2 * k + 1) * share]
                high = grad[(2 * k + 1) * share : (2 * k + 2) * share]
                send_ref[p, 0:share, lanes] = jnp.where(side == 0, high, low).astype(BF16)
                keep_ref[p, 0:share, lanes] = jnp.where(side == 0, low, high).astype(BF16)
                send_ref[p, share:, lanes] = empty
                keep_ref[p, share:, lanes] = empty
        for store in stores:
            store.wait()

    return kernel


def tiles_kernel(rows_ref, cols_ref, vals_ref, pushed_ref, dp_ref, ws_ref, out_ref, adj_ref):
    count, block, _ = vals_ref.shape
    adj_ref[...] = jnp.zeros_like(adj_ref)

    def add(t, carry):
        rows = pl.ds(pl.multiple_of(rows_ref[t] * block, block), block)
        cols = pl.ds(pl.multiple_of(cols_ref[t] * block, block), block)
        adj_ref[rows, cols] += vals_ref[t].astype(F32)
        return carry

    lax.fori_loop(0, count, add, 0)
    interior_t = dot_nn(pushed_ref[...], adj_ref[...].astype(BF16))
    out_ref[...] = dot_nt(dp_ref[...], ws_ref[...]) + interior_t.T


def member_sum_kernel(parts_ref, out_ref):
    total = jnp.sum(parts_ref[...].astype(F32), axis=0)
    half = out_ref.shape[2]
    out_ref[:, 0, :] = total[:, :half].astype(BF16)
    out_ref[:, 1, :] = total[:, half:].astype(BF16)


def grad_row_kernel(arrived_ref, out_ref):
    half = out_ref.shape[2]
    row = jnp.sum(arrived_ref[:, 1, half:].astype(F32), axis=0, keepdims=True).astype(BF16)
    for k in range(2):
        out_ref[:, k, :] = jnp.broadcast_to(row[:, k * half : (k + 1) * half], (out_ref.shape[0], half))


def finish_kernel(arrived_ref, target_ref, base_ref, out_ref):
    nodes, width = out_ref.shape
    groups = arrived_ref.shape[0]
    per_owner = target_ref.shape[0]
    arrived = jnp.concatenate([arrived_ref[:, 0, :], arrived_ref[:, 1, :]], axis=1)
    total = base_ref[...]
    for j in range(per_owner):
        node = lax.broadcasted_iota(jnp.int32, (nodes, groups), 0)
        put = jnp.where(node == target_ref[j : j + 1, :], 1.0, 0.0).astype(BF16)
        total += dot_nn(put, arrived[:, j * width : (j + 1) * width])
    out_ref[...] = total.astype(BF16)


def widen_kernel(grads_ref, self_ref, neigh_ref):
    members, share, _, half = grads_ref.shape
    for m in range(members):
        ref = (self_ref, neigh_ref)[2 * m // members]
        first = m % (members // 2) * share
        for k in range(2):
            ref[first : first + share, k * half : (k + 1) * half] = grads_ref[m, :, k, :].astype(F32)


def on_device(
    features,
    aggregate,
    preact,
    cotangent,
    w_self,
    w_neigh,
    tile_vals,
    tile_rows,
    tile_cols,
    edge_dst,
    edge_slot,
    edge_weight,
    recv_rows,
):
    groups = lax.axis_size("group")
    members = lax.axis_size("local")
    nodes, width = features.shape
    edges = edge_dst.shape[0]
    per_owner = recv_rows.shape[2]
    scale = (nodes * groups * members) ** (-0.5)
    payload = (per_owner + 1) * width
    share = 2 * width // members
    params = pltpu.CompilerParams(vmem_limit_bytes=VMEM_LIMIT)
    smem = pl.BlockSpec(memory_space=pltpu.SMEM)
    vmem = pl.BlockSpec(memory_space=pltpu.VMEM)
    hbm = pl.BlockSpec(memory_space=pltpu.HBM)

    operands = (
        edge_dst.reshape(1, edges),
        edge_slot.reshape(1, edges),
        edge_weight.reshape(1, edges),
        preact,
        cotangent,
        w_neigh,
        features,
        aggregate,
    )
    half = jax.ShapeDtypeStruct((members // 2, groups, payload), BF16)
    dp, pushed_t, send, keep = pl.pallas_call(
        edges_and_grads(groups, members, per_owner, scale, 512),
        out_shape=(
            pltpu.HBM((nodes, width), BF16),
            pltpu.HBM((width, nodes), BF16),
            half,
            half,
        ),
        in_specs=[hbm] * len(operands),
        out_specs=(hbm, hbm, vmem, vmem),
        scratch_shapes=[pltpu.VMEM(a.shape, a.dtype) for a in operands]
        + [
            pltpu.VMEM((nodes, width), BF16),
            pltpu.VMEM((width, nodes), BF16),
            pltpu.VMEM((members * per_owner, groups, edges), BF16),
            pltpu.SemaphoreType.DMA((len(operands),)),
            pltpu.SemaphoreType.DMA((2,)),
        ],
        compiler_params=params,
        name="edges_and_grads",
    )(*[pltpu.with_memory_space_constraint(a, pltpu.HBM) for a in operands])
    base = pl.pallas_call(
        tiles_kernel,
        out_shape=jax.ShapeDtypeStruct((nodes, width), F32),
        in_specs=[smem, smem, vmem, vmem, vmem, vmem],
        out_specs=vmem,
        scratch_shapes=[pltpu.VMEM((nodes, nodes), F32)],
        compiler_params=params,
        name="tiles",
    )(tile_rows, tile_cols, tile_vals, pushed_t, dp, w_self)

    other_core = [(i, i ^ 1) for i in range(members)]
    along_x = [list(range(core, members, 2)) for core in range(2)]
    came = lax.ppermute(send, "local", other_core)
    chip_sum = (came.astype(F32) + keep.astype(F32)).astype(BF16)
    parts = lax.all_to_all(chip_sum, "local", 0, 0, axis_index_groups=along_x, tiled=True)
    summed = pl.pallas_call(
        member_sum_kernel,
        out_shape=jax.ShapeDtypeStruct((groups, 2, payload // 2), BF16),
        compiler_params=params,
        name="member_sum",
    )(parts)
    arrived = lax.all_to_all(summed, "group", 0, 0, tiled=True)
    rows = pl.pallas_call(
        grad_row_kernel,
        out_shape=jax.ShapeDtypeStruct((groups, 2, width // 2), BF16),
        compiler_params=params,
        name="grad_row",
    )(arrived)
    rows, base = lax.optimization_barrier((rows, base))
    spread = lax.all_to_all(rows, "group", 0, 0, tiled=True)
    grad_x = pl.pallas_call(
        finish_kernel,
        out_shape=jax.ShapeDtypeStruct((nodes, width), BF16),
        compiler_params=params,
        name="finish",
    )(arrived, recv_rows.reshape(groups, per_owner).T, base)
    spread, grad_x = lax.optimization_barrier((spread, grad_x))
    mine = jnp.broadcast_to(spread[None, :share], (members, share, 2, width // 2))
    grads = lax.all_to_all(mine, "local", 0, 0, tiled=True)
    grad_self, grad_neigh = pl.pallas_call(
        widen_kernel,
        out_shape=(jax.ShapeDtypeStruct((width, width), F32), jax.ShapeDtypeStruct((width, width), F32)),
        compiler_params=params,
        name="widen",
    )(grads)
    return (grad_x, grad_self, grad_neigh)


def solution(mesh):
    both = ("group", "local")
    placed = (
        P(both, None),
        P(both, None),
        P(both, None),
        P(both, None),
        P(),
        P(),
        P(both, None, None),
        P(both),
        P(both),
        P(both),
        P(both),
        P(both),
        P("group", None, "local"),
    )
    return jax.shard_map(
        on_device,
        mesh=mesh,
        in_specs=placed,
        out_specs=(P(both, None), P(), P()),
        check_vma=False,
    )
```

```python
import jax
import jax.numpy as jnp
from jax import lax
from jax.experimental import pallas as pl
from jax.experimental.pallas import tpu as pltpu
from jax.sharding import PartitionSpec as P

F32 = jnp.float32
BF16 = jnp.bfloat16
VMEM_LIMIT = 24 * 1024 * 1024


def dot_nn(first_op, second_op):
    return lax.dot_general(first_op, second_op, (((1,), (0,)), ((), ())), preferred_element_type=F32)


def dot_nt(first_op, second_op):
    return lax.dot_general(first_op, second_op, (((1,), (1,)), ((), ())), preferred_element_type=F32)


def dot_tn(first_op, second_op):
    return lax.dot_general(first_op, second_op, (((0,), (0,)), ((), ())), preferred_element_type=F32)


def one_hot(index, count):
    row = lax.broadcasted_iota(jnp.int16, (count, index.shape[1]), 0)
    return jnp.where(row == index.astype(jnp.int16), jnp.ones((), BF16), jnp.zeros((), BF16))


def edges_and_grads(groups, members, per_owner, scale, chunk):
    def kernel(
        dst_hbm, slot_hbm, weight_hbm, preact_hbm, cot_hbm, wn_hbm, feat_hbm, agg_hbm,
        dp_hbm, pushed_hbm, send_ref, keep_ref,
        dst_ref, slot_ref, weight_ref, preact_ref, cot_ref, wn_ref, feat_ref, agg_ref,
        dp_ref, pushed_ref, put_ref, in_sem, out_sem,
    ):
        sources = (dst_hbm, slot_hbm, weight_hbm, preact_hbm, cot_hbm, wn_hbm, feat_hbm, agg_hbm)
        held = (dst_ref, slot_ref, weight_ref, preact_ref, cot_ref, wn_ref, feat_ref, agg_ref)
        loads = [pltpu.make_async_copy(s, d, in_sem.at[i]) for i, (s, d) in enumerate(zip(sources, held))]
        for load in loads:
            load.start()
        nodes, width = preact_ref.shape
        edges = dst_ref.shape[1]
        side = lax.rem(lax.axis_index("local"), 2)
        for load in loads[:3]:
            load.wait()
        slot = slot_ref[...]
        per_group = members * per_owner
        rows = members * groups
        group = slot // per_group
        rest = slot - group * per_group
        member = rest // per_owner
        which = rest - member * per_owner
        place = which * rows + member * groups + group
        pieces = [
            (ref, j, p, j * rows + (2 * p + parity) * groups)
            for ref, parity in ((send_ref, 1 - side), (keep_ref, side))
            for j in range(per_owner)
            for p in range(members // 2)
        ]
        for n, (_, _, _, first) in enumerate(pieces):
            put_ref[n * groups : (n + 1) * groups, :] = one_hot(place - first, groups)
        for load in loads[3:6]:
            load.wait()
        x = preact_ref[...].astype(F32)
        sig = jax.nn.sigmoid(x)
        dp = (cot_ref[...].astype(F32) * sig * (1.0 + x * (1.0 - sig))).astype(BF16)
        dp_ref[...] = dp
        pushed_t = dot_nt(wn_ref[...], dp).astype(BF16)
        pushed_ref[...] = pushed_t
        stores = [
            pltpu.make_async_copy(dp_ref, dp_hbm, out_sem.at[0]),
            pltpu.make_async_copy(pushed_ref, pushed_hbm, out_sem.at[1]),
        ]
        for store in stores:
            store.start()

        all_terms = []
        for e0 in range(0, edges, chunk):
            dst = dst_ref[:, e0 : e0 + chunk]
            take = one_hot(dst, nodes)
            all_terms.append((dot_nn(pushed_t, take) * weight_ref[:, e0 : e0 + chunk]).astype(BF16))
        terms = jnp.concatenate(all_terms, axis=1)

        sums = dot_nt(put_ref[...], terms).astype(BF16)
        for n, (ref, j, p, _) in enumerate(pieces):
            ref[p, :, j * width : (j + 1) * width] = sums[n * groups : (n + 1) * groups]

        for load in loads[6:]:
            load.wait()
        share = 2 * width // members
        empty = jnp.zeros((groups - share, width), BF16)
        lanes = slice(per_owner * width, (per_owner + 1) * width)
        for i, ref in enumerate((feat_ref, agg_ref)):
            grad = dot_tn(ref[...], dp) * scale
            for k in range(members // 4):
                p = i * (members // 4) + k
                low = grad[2 * k * share : (2 * k + 1) * share]
                high = grad[(2 * k + 1) * share : (2 * k + 2) * share]
                send_ref[p, 0:share, lanes] = jnp.where(side == 0, high, low).astype(BF16)
                keep_ref[p, 0:share, lanes] = jnp.where(side == 0, low, high).astype(BF16)
                send_ref[p, share:, lanes] = empty
                keep_ref[p, share:, lanes] = empty
        for store in stores:
            store.wait()

    return kernel


def tiles_kernel(
    rows_ref, cols_ref, vals_ref, pushed_hbm, dp_hbm, ws_ref, out_ref, adj_ref, pushed_ref, dp_ref, in_sem
):
    loads = [
        pltpu.make_async_copy(pushed_hbm, pushed_ref, in_sem.at[0]),
        pltpu.make_async_copy(dp_hbm, dp_ref, in_sem.at[1]),
    ]
    for load in loads:
        load.start()
    count, block, _ = vals_ref.shape
    adj_ref[...] = jnp.zeros_like(adj_ref)

    def add(t, carry):
        rows = pl.ds(pl.multiple_of(rows_ref[t] * block, block), block)
        cols = pl.ds(pl.multiple_of(cols_ref[t] * block, block), block)
        adj_ref[rows, cols] += vals_ref[t].astype(F32)
        return carry

    lax.fori_loop(0, count, add, 0)
    for load in loads:
        load.wait()
    interior_t = dot_nn(pushed_ref[...], adj_ref[...].astype(BF16))
    out_ref[...] = dot_nt(dp_ref[...], ws_ref[...]) + interior_t.T


def member_sum_kernel(parts_ref, out_ref):
    total = jnp.sum(parts_ref[...].astype(F32), axis=0)
    half = out_ref.shape[2]
    out_ref[:, 0, :] = total[:, :half].astype(BF16)
    out_ref[:, 1, :] = total[:, half:].astype(BF16)


def grad_row_kernel(arrived_ref, out_ref):
    half = out_ref.shape[2]
    row = jnp.sum(arrived_ref[:, 1, half:].astype(F32), axis=0, keepdims=True).astype(BF16)
    for k in range(2):
        out_ref[:, k, :] = jnp.broadcast_to(row[:, k * half : (k + 1) * half], (out_ref.shape[0], half))


def finish_kernel(arrived_ref, target_ref, base_ref, out_ref):
    nodes, width = out_ref.shape
    groups = arrived_ref.shape[0]
    per_owner = target_ref.shape[0]
    arrived = jnp.concatenate([arrived_ref[:, 0, :], arrived_ref[:, 1, :]], axis=1)
    total = base_ref[...]
    for j in range(per_owner):
        total += dot_nn(one_hot(target_ref[j : j + 1, :], nodes), arrived[:, j * width : (j + 1) * width])
    out_ref[...] = total.astype(BF16)


def widen_kernel(grads_ref, self_ref, neigh_ref):
    members, share, _, half = grads_ref.shape
    for m in range(members):
        ref = (self_ref, neigh_ref)[2 * m // members]
        first = m % (members // 2) * share
        for k in range(2):
            ref[first : first + share, k * half : (k + 1) * half] = grads_ref[m, :, k, :].astype(F32)


def on_device(
    features,
    aggregate,
    preact,
    cotangent,
    w_self,
    w_neigh,
    tile_vals,
    tile_rows,
    tile_cols,
    edge_dst,
    edge_slot,
    edge_weight,
    recv_rows,
):
    groups = lax.axis_size("group")
    members = lax.axis_size("local")
    nodes, width = features.shape
    edges = edge_dst.shape[0]
    per_owner = recv_rows.shape[2]
    scale = (nodes * groups * members) ** (-0.5)
    payload = (per_owner + 1) * width
    share = 2 * width // members
    params = pltpu.CompilerParams(vmem_limit_bytes=VMEM_LIMIT)
    smem = pl.BlockSpec(memory_space=pltpu.SMEM)
    vmem = pl.BlockSpec(memory_space=pltpu.VMEM)
    hbm = pl.BlockSpec(memory_space=pltpu.HBM)

    operands = (
        edge_dst.reshape(1, edges),
        edge_slot.reshape(1, edges),
        edge_weight.reshape(1, edges),
        preact,
        cotangent,
        w_neigh,
        features,
        aggregate,
    )
    half = jax.ShapeDtypeStruct((members // 2, groups, payload), BF16)
    dp, pushed_t, send, keep = pl.pallas_call(
        edges_and_grads(groups, members, per_owner, scale, 512),
        out_shape=(
            pltpu.HBM((nodes, width), BF16),
            pltpu.HBM((width, nodes), BF16),
            half,
            half,
        ),
        in_specs=[hbm] * len(operands),
        out_specs=(hbm, hbm, vmem, vmem),
        scratch_shapes=[pltpu.VMEM(a.shape, a.dtype) for a in operands]
        + [
            pltpu.VMEM((nodes, width), BF16),
            pltpu.VMEM((width, nodes), BF16),
            pltpu.VMEM((members * per_owner * groups, edges), BF16),
            pltpu.SemaphoreType.DMA((len(operands),)),
            pltpu.SemaphoreType.DMA((2,)),
        ],
        compiler_params=params,
        name="edges_and_grads",
    )(*[pltpu.with_memory_space_constraint(a, pltpu.HBM) for a in operands])
    base = pl.pallas_call(
        tiles_kernel,
        out_shape=jax.ShapeDtypeStruct((nodes, width), F32),
        in_specs=[smem, smem, vmem, hbm, hbm, vmem],
        out_specs=vmem,
        scratch_shapes=[
            pltpu.VMEM((nodes, nodes), F32),
            pltpu.VMEM((width, nodes), BF16),
            pltpu.VMEM((nodes, width), BF16),
            pltpu.SemaphoreType.DMA((2,)),
        ],
        compiler_params=params,
        name="tiles",
    )(
        tile_rows,
        tile_cols,
        tile_vals,
        pltpu.with_memory_space_constraint(pushed_t, pltpu.HBM),
        pltpu.with_memory_space_constraint(dp, pltpu.HBM),
        w_self,
    )

    other_core = [(i, i ^ 1) for i in range(members)]
    along_x = [list(range(core, members, 2)) for core in range(2)]
    came = lax.ppermute(send, "local", other_core)
    chip_sum = (came.astype(F32) + keep.astype(F32)).astype(BF16)
    parts = lax.all_to_all(chip_sum, "local", 0, 0, axis_index_groups=along_x, tiled=True)
    summed = pl.pallas_call(
        member_sum_kernel,
        out_shape=jax.ShapeDtypeStruct((groups, 2, payload // 2), BF16),
        compiler_params=params,
        name="member_sum",
    )(parts)
    arrived = lax.all_to_all(summed, "group", 0, 0, tiled=True)
    rows = pl.pallas_call(
        grad_row_kernel,
        out_shape=jax.ShapeDtypeStruct((groups, 2, width // 2), BF16),
        compiler_params=params,
        name="grad_row",
    )(arrived)
    rows, base = lax.optimization_barrier((rows, base))
    spread = lax.all_to_all(rows, "group", 0, 0, tiled=True)
    grad_x = pl.pallas_call(
        finish_kernel,
        out_shape=jax.ShapeDtypeStruct((nodes, width), BF16),
        compiler_params=params,
        name="finish",
    )(arrived, recv_rows.reshape(groups, per_owner).T, base)
    spread, grad_x = lax.optimization_barrier((spread, grad_x))
    mine = jnp.broadcast_to(spread[None, :share], (members, share, 2, width // 2))
    grads = lax.all_to_all(mine, "local", 0, 0, tiled=True)
    grad_self, grad_neigh = pl.pallas_call(
        widen_kernel,
        out_shape=(jax.ShapeDtypeStruct((width, width), F32), jax.ShapeDtypeStruct((width, width), F32)),
        compiler_params=params,
        name="widen",
    )(grads)
    return (grad_x, grad_self, grad_neigh)


def solution(mesh):
    both = ("group", "local")
    placed = (
        P(both, None),
        P(both, None),
        P(both, None),
        P(both, None),
        P(),
        P(),
        P(both, None, None),
        P(both),
        P(both),
        P(both),
        P(both),
        P(both),
        P("group", None, "local"),
    )
    return jax.shard_map(
        on_device,
        mesh=mesh,
        in_specs=placed,
        out_specs=(P(both, None), P(), P()),
        check_vma=False,
    )
```

```python
import jax
import jax.numpy as jnp
from jax import lax
from jax.experimental import pallas as pl
from jax.experimental.pallas import tpu as pltpu
from jax.sharding import PartitionSpec as P

F32 = jnp.float32
BF16 = jnp.bfloat16
VMEM_LIMIT = 24 * 1024 * 1024
OWNERS = 16


def dot_nn(first_op, second_op):
    return lax.dot_general(first_op, second_op, (((1,), (0,)), ((), ())), preferred_element_type=F32)


def dot_nt(first_op, second_op):
    return lax.dot_general(first_op, second_op, (((1,), (1,)), ((), ())), preferred_element_type=F32)


def dot_tn(first_op, second_op):
    return lax.dot_general(first_op, second_op, (((0,), (0,)), ((), ())), preferred_element_type=F32)


def one_hot(index, count):
    row = lax.broadcasted_iota(jnp.int16, (count, index.shape[1]), 0)
    return jnp.where(row == index.astype(jnp.int16), jnp.ones((), BF16), jnp.zeros((), BF16))


def edges_and_grads(groups, members, per_owner, scale, chunk):
    def kernel(
        dst_hbm, slot_hbm, weight_hbm, preact_hbm, cot_hbm, wn_hbm, feat_hbm, agg_hbm,
        dp_hbm, pushed_hbm, send_ref, keep_ref,
        dst_ref, slot_ref, weight_ref, preact_ref, cot_ref, wn_ref, feat_ref, agg_ref,
        dp_ref, pushed_ref, put_ref, in_sem, out_sem,
    ):
        sources = (dst_hbm, slot_hbm, weight_hbm, preact_hbm, cot_hbm, wn_hbm, feat_hbm, agg_hbm)
        held = (dst_ref, slot_ref, weight_ref, preact_ref, cot_ref, wn_ref, feat_ref, agg_ref)
        loads = [pltpu.make_async_copy(s, d, in_sem.at[i]) for i, (s, d) in enumerate(zip(sources, held))]
        for load in loads:
            load.start()
        nodes, width = preact_ref.shape
        edges = dst_ref.shape[1]
        side = lax.rem(lax.axis_index("local"), 2)
        for load in loads[:3]:
            load.wait()
        slot = slot_ref[...]
        per_group = members * per_owner
        rows = members * groups
        group = slot // per_group
        rest = slot - group * per_group
        member = rest // per_owner
        which = rest - member * per_owner
        place = which * rows + member * groups + group
        pieces = [
            (ref, j, p, j * rows + (2 * p + parity) * groups)
            for ref, parity in ((send_ref, 1 - side), (keep_ref, side))
            for j in range(per_owner)
            for p in range(members // 2)
        ]
        for n, (_, _, _, first) in enumerate(pieces):
            put_ref[n * groups : (n + 1) * groups, :] = one_hot(place - first, groups)
        for load in loads[3:6]:
            load.wait()
        x = preact_ref[...].astype(F32)
        sig = jax.nn.sigmoid(x)
        dp = (cot_ref[...].astype(F32) * sig * (1.0 + x * (1.0 - sig))).astype(BF16)
        dp_ref[...] = dp
        pushed_t = dot_nt(wn_ref[...], dp).astype(BF16)
        pushed_ref[...] = pushed_t
        stores = [
            pltpu.make_async_copy(dp_ref, dp_hbm, out_sem.at[0]),
            pltpu.make_async_copy(pushed_ref, pushed_hbm, out_sem.at[1]),
        ]
        for store in stores:
            store.start()

        all_terms = []
        for e0 in range(0, edges, chunk):
            dst = dst_ref[:, e0 : e0 + chunk]
            take = one_hot(dst, nodes)
            all_terms.append((dot_nn(pushed_t, take) * weight_ref[:, e0 : e0 + chunk]).astype(BF16))
        terms = jnp.concatenate(all_terms, axis=1)

        sums = dot_nt(put_ref[...], terms).astype(BF16)
        for n, (ref, j, p, _) in enumerate(pieces):
            ref[p, j * groups : (j + 1) * groups] = sums[n * groups : (n + 1) * groups]

        for load in loads[6:]:
            load.wait()
        share = 2 * width // members
        tail = slice(per_owner * groups, per_owner * groups + share)
        for i, ref in enumerate((feat_ref, agg_ref)):
            grad = dot_tn(ref[...], dp) * scale
            for k in range(members // 4):
                p = i * (members // 4) + k
                low = grad[2 * k * share : (2 * k + 1) * share]
                high = grad[(2 * k + 1) * share : (2 * k + 2) * share]
                send_ref[p, tail] = jnp.where(side == 0, high, low).astype(BF16)
                keep_ref[p, tail] = jnp.where(side == 0, low, high).astype(BF16)
        for store in stores:
            store.wait()

    return kernel


def tiles_kernel(
    rows_ref, cols_ref, vals_ref, pushed_hbm, dp_hbm, ws_ref, out_ref, adj_ref, pushed_ref, dp_ref, in_sem
):
    loads = [
        pltpu.make_async_copy(pushed_hbm, pushed_ref, in_sem.at[0]),
        pltpu.make_async_copy(dp_hbm, dp_ref, in_sem.at[1]),
    ]
    for load in loads:
        load.start()
    count, block, _ = vals_ref.shape
    adj_ref[...] = jnp.zeros_like(adj_ref)

    def add(t, carry):
        rows = pl.ds(pl.multiple_of(rows_ref[t] * block, block), block)
        cols = pl.ds(pl.multiple_of(cols_ref[t] * block, block), block)
        adj_ref[rows, cols] += vals_ref[t].astype(F32)
        return carry

    lax.fori_loop(0, count, add, 0)
    for load in loads:
        load.wait()
    interior_t = dot_nn(pushed_ref[...], adj_ref[...].astype(BF16))
    out_ref[...] = dot_nt(dp_ref[...], ws_ref[...]) + interior_t.T


def member_sum(per_owner, owners):
    def kernel(parts_ref, out_ref):
        total = jnp.sum(parts_ref[...].astype(F32), axis=0).astype(BF16)
        groups = out_ref.shape[0]
        width = total.shape[1]
        pieces = [total[j * groups : (j + 1) * groups] for j in range(per_owner)]
        for first in range(per_owner * groups, total.shape[0], owners):
            pieces.append(jnp.concatenate([total[first : first + owners]] * (groups // owners), axis=0))
        per_line = len(pieces) // 2
        for n, piece in enumerate(pieces):
            k, at = n // per_line, n % per_line * width
            out_ref[:, k, at : at + width] = piece

    return kernel


def grad_rows(per_owner, width):
    def kernel(arrived_ref, out_ref):
        per_line = arrived_ref.shape[2] // width
        owners, lines, lanes = out_ref.shape
        rows = []
        for n in range(per_owner, 2 * per_line):
            k, at = n // per_line, n % per_line * width
            row = jnp.sum(arrived_ref[:, k, at : at + width].astype(F32), axis=0, keepdims=True)
            rows += [row[:, h : h + lanes] for h in range(0, width, lanes)]
        tile = jnp.concatenate(rows, axis=0)
        out_ref[...] = jnp.broadcast_to(tile[None], (owners, lines, lanes)).astype(BF16)

    return kernel


def finish_kernel(arrived_ref, target_ref, base_ref, out_ref):
    nodes, width = out_ref.shape
    total = base_ref[...]
    for j in range(target_ref.shape[0]):
        put = one_hot(target_ref[j : j + 1, :], nodes)
        total += dot_nn(put, arrived_ref[:, 0, j * width : (j + 1) * width])
    out_ref[...] = total.astype(BF16)


def widen_kernel(grads_ref, self_ref, neigh_ref):
    members, owners, lines, lanes = grads_ref.shape
    per_row = self_ref.shape[1] // lanes
    share = owners * lines // per_row
    for m in range(members):
        ref = (self_ref, neigh_ref)[2 * m // members]
        first = m % (members // 2) * share
        part = grads_ref[m].astype(F32)
        for n in range(lines):
            at, col = first + n // per_row * owners, n % per_row * lanes
            ref[at : at + owners, col : col + lanes] = part[:, n, :]


def on_device(
    features,
    aggregate,
    preact,
    cotangent,
    w_self,
    w_neigh,
    tile_vals,
    tile_rows,
    tile_cols,
    edge_dst,
    edge_slot,
    edge_weight,
    recv_rows,
):
    groups = lax.axis_size("group")
    members = lax.axis_size("local")
    nodes, width = features.shape
    edges = edge_dst.shape[0]
    per_owner = recv_rows.shape[2]
    scale = (nodes * groups * members) ** (-0.5)
    share = 2 * width // members
    rows_held = share // OWNERS
    payload = (per_owner + rows_held) * width
    lines = rows_held * width // 128
    params = pltpu.CompilerParams(vmem_limit_bytes=VMEM_LIMIT)
    smem = pl.BlockSpec(memory_space=pltpu.SMEM)
    vmem = pl.BlockSpec(memory_space=pltpu.VMEM)
    hbm = pl.BlockSpec(memory_space=pltpu.HBM)

    operands = (
        edge_dst.reshape(1, edges),
        edge_slot.reshape(1, edges),
        edge_weight.reshape(1, edges),
        preact,
        cotangent,
        w_neigh,
        features,
        aggregate,
    )
    half = jax.ShapeDtypeStruct((members // 2, per_owner * groups + share, width), BF16)
    dp, pushed_t, send, keep = pl.pallas_call(
        edges_and_grads(groups, members, per_owner, scale, 512),
        out_shape=(
            pltpu.HBM((nodes, width), BF16),
            pltpu.HBM((width, nodes), BF16),
            half,
            half,
        ),
        in_specs=[hbm] * len(operands),
        out_specs=(hbm, hbm, vmem, vmem),
        scratch_shapes=[pltpu.VMEM(a.shape, a.dtype) for a in operands]
        + [
            pltpu.VMEM((nodes, width), BF16),
            pltpu.VMEM((width, nodes), BF16),
            pltpu.VMEM((members * per_owner * groups, edges), BF16),
            pltpu.SemaphoreType.DMA((len(operands),)),
            pltpu.SemaphoreType.DMA((2,)),
        ],
        compiler_params=params,
        name="edges_and_grads",
    )(*[pltpu.with_memory_space_constraint(a, pltpu.HBM) for a in operands])
    base = pl.pallas_call(
        tiles_kernel,
        out_shape=jax.ShapeDtypeStruct((nodes, width), F32),
        in_specs=[smem, smem, vmem, hbm, hbm, vmem],
        out_specs=vmem,
        scratch_shapes=[
            pltpu.VMEM((nodes, nodes), F32),
            pltpu.VMEM((width, nodes), BF16),
            pltpu.VMEM((nodes, width), BF16),
            pltpu.SemaphoreType.DMA((2,)),
        ],
        compiler_params=params,
        name="tiles",
    )(
        tile_rows,
        tile_cols,
        tile_vals,
        pltpu.with_memory_space_constraint(pushed_t, pltpu.HBM),
        pltpu.with_memory_space_constraint(dp, pltpu.HBM),
        w_self,
    )

    other_core = [(i, i ^ 1) for i in range(members)]
    along_x = [list(range(core, members, 2)) for core in range(2)]
    came = lax.ppermute(send, "local", other_core)
    chip_sum = (came.astype(F32) + keep.astype(F32)).astype(BF16)
    parts = lax.all_to_all(chip_sum, "local", 0, 0, axis_index_groups=along_x, tiled=True)
    summed = pl.pallas_call(
        member_sum(per_owner, OWNERS),
        out_shape=jax.ShapeDtypeStruct((groups, 2, payload // 2), BF16),
        compiler_params=params,
        name="member_sum",
    )(parts)
    arrived = lax.all_to_all(summed, "group", 0, 0, tiled=True)
    rows = pl.pallas_call(
        grad_rows(per_owner, width),
        out_shape=jax.ShapeDtypeStruct((OWNERS, lines, 128), BF16),
        compiler_params=params,
        name="grad_rows",
    )(arrived)
    rows, base = lax.optimization_barrier((rows, base))
    blocks = [list(range(first, first + OWNERS)) for first in range(0, groups, OWNERS)]
    spread = lax.all_to_all(rows, "group", 0, 0, axis_index_groups=blocks, tiled=True)
    grad_x = pl.pallas_call(
        finish_kernel,
        out_shape=jax.ShapeDtypeStruct((nodes, width), BF16),
        compiler_params=params,
        name="finish",
    )(arrived, recv_rows.reshape(groups, per_owner).T, base)
    spread, grad_x = lax.optimization_barrier((spread, grad_x))
    mine = jnp.broadcast_to(spread[None], (members, OWNERS, lines, 128))
    grads = lax.all_to_all(mine, "local", 0, 0, tiled=True)
    grad_self, grad_neigh = pl.pallas_call(
        widen_kernel,
        out_shape=(jax.ShapeDtypeStruct((width, width), F32), jax.ShapeDtypeStruct((width, width), F32)),
        compiler_params=params,
        name="widen",
    )(grads)
    return (grad_x, grad_self, grad_neigh)


def solution(mesh):
    both = ("group", "local")
    placed = (
        P(both, None),
        P(both, None),
        P(both, None),
        P(both, None),
        P(),
        P(),
        P(both, None, None),
        P(both),
        P(both),
        P(both),
        P(both),
        P(both),
        P("group", None, "local"),
    )
    return jax.shard_map(
        on_device,
        mesh=mesh,
        in_specs=placed,
        out_specs=(P(both, None), P(), P()),
        check_vma=False,
    )
```

```python
import jax
import jax.numpy as jnp
from jax import lax
from jax.experimental import pallas as pl
from jax.experimental.pallas import tpu as pltpu
from jax.sharding import PartitionSpec as P

F32 = jnp.float32
BF16 = jnp.bfloat16
VMEM_LIMIT = 24 * 1024 * 1024
OWNERS = 16


def dot_nn(first_op, second_op):
    return lax.dot_general(first_op, second_op, (((1,), (0,)), ((), ())), preferred_element_type=F32)


def dot_nt(first_op, second_op):
    return lax.dot_general(first_op, second_op, (((1,), (1,)), ((), ())), preferred_element_type=F32)


def dot_tn(first_op, second_op):
    return lax.dot_general(first_op, second_op, (((0,), (0,)), ((), ())), preferred_element_type=F32)


def one_hot(index, count):
    row = lax.broadcasted_iota(jnp.int16, (count, index.shape[1]), 0)
    return jnp.where(row == index.astype(jnp.int16), jnp.ones((), BF16), jnp.zeros((), BF16))


def fill_slots(put_ref, place, parity, groups, members, per_owner):
    for j in range(per_owner):
        for p in range(members // 2):
            first = j * members * groups + (2 * p + parity) * groups
            at = (j * (members // 2) + p) * groups
            put_ref[at : at + groups, :] = one_hot(place - first, groups)


def store_slots(ref, sums, groups, per_owner):
    sums = sums.astype(BF16)
    for j in range(per_owner):
        for p in range(ref.shape[0]):
            at = (j * ref.shape[0] + p) * groups
            ref[p, j * groups : (j + 1) * groups] = sums[at : at + groups]


def edges_and_grads(groups, members, per_owner, scale, chunk):
    def kernel(
        dst_hbm, slot_hbm, weight_hbm, preact_hbm, cot_hbm, wn_hbm, feat_hbm, agg_hbm,
        dp_hbm, pushed_hbm, send_ref, tail_ref, terms_ref, place_ref,
        dst_ref, slot_ref, weight_ref, preact_ref, cot_ref, wn_ref, feat_ref, agg_ref,
        dp_ref, pushed_ref, put_ref, in_sem, out_sem,
    ):
        sources = (dst_hbm, slot_hbm, weight_hbm, preact_hbm, cot_hbm, wn_hbm, feat_hbm, agg_hbm)
        held = (dst_ref, slot_ref, weight_ref, preact_ref, cot_ref, wn_ref, feat_ref, agg_ref)
        loads = [pltpu.make_async_copy(s, d, in_sem.at[i]) for i, (s, d) in enumerate(zip(sources, held))]
        for load in loads:
            load.start()
        nodes, width = preact_ref.shape
        edges = dst_ref.shape[1]
        side = lax.rem(lax.axis_index("local"), 2)
        for load in loads[:3]:
            load.wait()
        slot = slot_ref[...]
        per_group = members * per_owner
        rows = members * groups
        group = slot // per_group
        rest = slot - group * per_group
        member = rest // per_owner
        which = rest - member * per_owner
        place = which * rows + member * groups + group
        place_ref[...] = place
        fill_slots(put_ref, place, 1 - side, groups, members, per_owner)
        for load in loads[3:6]:
            load.wait()
        x = preact_ref[...].astype(F32)
        sig = jax.nn.sigmoid(x)
        dp = (cot_ref[...].astype(F32) * sig * (1.0 + x * (1.0 - sig))).astype(BF16)
        dp_ref[...] = dp
        pushed_t = dot_nt(wn_ref[...], dp).astype(BF16)
        pushed_ref[...] = pushed_t
        stores = [
            pltpu.make_async_copy(dp_ref, dp_hbm, out_sem.at[0]),
            pltpu.make_async_copy(pushed_ref, pushed_hbm, out_sem.at[1]),
        ]
        for store in stores:
            store.start()

        all_terms = []
        for e0 in range(0, edges, chunk):
            dst = dst_ref[:, e0 : e0 + chunk]
            take = one_hot(dst, nodes)
            all_terms.append((dot_nn(pushed_t, take) * weight_ref[:, e0 : e0 + chunk]).astype(BF16))
        terms = jnp.concatenate(all_terms, axis=1)
        terms_ref[...] = terms

        store_slots(send_ref, dot_nt(put_ref[...], terms), groups, per_owner)

        for load in loads[6:]:
            load.wait()
        share = 2 * width // members
        tail = slice(per_owner * groups, per_owner * groups + share)
        for i, ref in enumerate((feat_ref, agg_ref)):
            grad = dot_tn(ref[...], dp) * scale
            for k in range(members // 4):
                p = i * (members // 4) + k
                low = grad[2 * k * share : (2 * k + 1) * share]
                high = grad[(2 * k + 1) * share : (2 * k + 2) * share]
                send_ref[p, tail] = jnp.where(side == 0, high, low).astype(BF16)
                tail_ref[p] = jnp.where(side == 0, low, high).astype(BF16)
        for store in stores:
            store.wait()

    return kernel


def own_side(groups, members, per_owner):
    def kernel(terms_ref, place_ref, tail_ref, keep_ref, put_ref):
        side = lax.rem(lax.axis_index("local"), 2)
        fill_slots(put_ref, place_ref[...], side, groups, members, per_owner)
        store_slots(keep_ref, dot_nt(put_ref[...], terms_ref[...]), groups, per_owner)
        keep_ref[:, per_owner * groups :] = tail_ref[...]

    return kernel


def tiles_kernel(
    rows_ref, cols_ref, vals_ref, pushed_hbm, dp_hbm, ws_ref, out_ref, adj_ref, pushed_ref, dp_ref, in_sem
):
    loads = [
        pltpu.make_async_copy(pushed_hbm, pushed_ref, in_sem.at[0]),
        pltpu.make_async_copy(dp_hbm, dp_ref, in_sem.at[1]),
    ]
    for load in loads:
        load.start()
    count, block, _ = vals_ref.shape
    adj_ref[...] = jnp.zeros_like(adj_ref)

    def add(t, carry):
        rows = pl.ds(pl.multiple_of(rows_ref[t] * block, block), block)
        cols = pl.ds(pl.multiple_of(cols_ref[t] * block, block), block)
        adj_ref[rows, cols] += vals_ref[t].astype(F32)
        return carry

    lax.fori_loop(0, count, add, 0)
    for load in loads:
        load.wait()
    interior_t = dot_nn(pushed_ref[...], adj_ref[...].astype(BF16))
    out_ref[...] = dot_nt(dp_ref[...], ws_ref[...]) + interior_t.T


def member_sum(per_owner, owners):
    def kernel(parts_ref, out_ref):
        total = jnp.sum(parts_ref[...].astype(F32), axis=0).astype(BF16)
        groups = out_ref.shape[0]
        width = total.shape[1]
        pieces = [total[j * groups : (j + 1) * groups] for j in range(per_owner)]
        for first in range(per_owner * groups, total.shape[0], owners):
            pieces.append(jnp.concatenate([total[first : first + owners]] * (groups // owners), axis=0))
        per_line = len(pieces) // 2
        for n, piece in enumerate(pieces):
            k, at = n // per_line, n % per_line * width
            out_ref[:, k, at : at + width] = piece

    return kernel


def grad_rows(per_owner, width):
    def kernel(arrived_ref, out_ref):
        per_line = arrived_ref.shape[2] // width
        owners, lines, lanes = out_ref.shape
        rows = []
        for n in range(per_owner, 2 * per_line):
            k, at = n // per_line, n % per_line * width
            row = jnp.sum(arrived_ref[:, k, at : at + width].astype(F32), axis=0, keepdims=True)
            rows += [row[:, h : h + lanes] for h in range(0, width, lanes)]
        tile = jnp.concatenate(rows, axis=0)
        out_ref[...] = jnp.broadcast_to(tile[None], (owners, lines, lanes)).astype(BF16)

    return kernel


def finish_kernel(arrived_ref, target_ref, base_ref, out_ref):
    nodes, width = out_ref.shape
    total = base_ref[...]
    for j in range(target_ref.shape[0]):
        put = one_hot(target_ref[j : j + 1, :], nodes)
        total += dot_nn(put, arrived_ref[:, 0, j * width : (j + 1) * width])
    out_ref[...] = total.astype(BF16)


def widen_kernel(grads_ref, self_ref, neigh_ref):
    members, owners, lines, lanes = grads_ref.shape
    per_row = self_ref.shape[1] // lanes
    share = owners * lines // per_row
    for m in range(members):
        ref = (self_ref, neigh_ref)[2 * m // members]
        first = m % (members // 2) * share
        part = grads_ref[m].astype(F32)
        for n in range(lines):
            at, col = first + n // per_row * owners, n % per_row * lanes
            ref[at : at + owners, col : col + lanes] = part[:, n, :]


def on_device(
    features,
    aggregate,
    preact,
    cotangent,
    w_self,
    w_neigh,
    tile_vals,
    tile_rows,
    tile_cols,
    edge_dst,
    edge_slot,
    edge_weight,
    recv_rows,
):
    groups = lax.axis_size("group")
    members = lax.axis_size("local")
    nodes, width = features.shape
    edges = edge_dst.shape[0]
    per_owner = recv_rows.shape[2]
    scale = (nodes * groups * members) ** (-0.5)
    share = 2 * width // members
    rows_held = share // OWNERS
    payload = (per_owner + rows_held) * width
    lines = rows_held * width // 128
    params = pltpu.CompilerParams(vmem_limit_bytes=VMEM_LIMIT)
    smem = pl.BlockSpec(memory_space=pltpu.SMEM)
    vmem = pl.BlockSpec(memory_space=pltpu.VMEM)
    hbm = pl.BlockSpec(memory_space=pltpu.HBM)

    operands = (
        edge_dst.reshape(1, edges),
        edge_slot.reshape(1, edges),
        edge_weight.reshape(1, edges),
        preact,
        cotangent,
        w_neigh,
        features,
        aggregate,
    )
    half = jax.ShapeDtypeStruct((members // 2, per_owner * groups + share, width), BF16)
    dp, pushed_t, send, tail, terms, place = pl.pallas_call(
        edges_and_grads(groups, members, per_owner, scale, 512),
        out_shape=(
            pltpu.HBM((nodes, width), BF16),
            pltpu.HBM((width, nodes), BF16),
            half,
            jax.ShapeDtypeStruct((members // 2, share, width), BF16),
            jax.ShapeDtypeStruct((width, edges), BF16),
            jax.ShapeDtypeStruct((1, edges), jnp.int32),
        ),
        in_specs=[hbm] * len(operands),
        out_specs=(hbm, hbm, vmem, vmem, vmem, vmem),
        scratch_shapes=[pltpu.VMEM(a.shape, a.dtype) for a in operands]
        + [
            pltpu.VMEM((nodes, width), BF16),
            pltpu.VMEM((width, nodes), BF16),
            pltpu.VMEM((members * per_owner * groups // 2, edges), BF16),
            pltpu.SemaphoreType.DMA((len(operands),)),
            pltpu.SemaphoreType.DMA((2,)),
        ],
        compiler_params=params,
        name="edges_and_grads",
    )(*[pltpu.with_memory_space_constraint(a, pltpu.HBM) for a in operands])
    base = pl.pallas_call(
        tiles_kernel,
        out_shape=jax.ShapeDtypeStruct((nodes, width), F32),
        in_specs=[smem, smem, vmem, hbm, hbm, vmem],
        out_specs=vmem,
        scratch_shapes=[
            pltpu.VMEM((nodes, nodes), F32),
            pltpu.VMEM((width, nodes), BF16),
            pltpu.VMEM((nodes, width), BF16),
            pltpu.SemaphoreType.DMA((2,)),
        ],
        compiler_params=params,
        name="tiles",
    )(
        tile_rows,
        tile_cols,
        tile_vals,
        pltpu.with_memory_space_constraint(pushed_t, pltpu.HBM),
        pltpu.with_memory_space_constraint(dp, pltpu.HBM),
        w_self,
    )

    other_core = [(i, i ^ 1) for i in range(members)]
    along_x = [list(range(core, members, 2)) for core in range(2)]
    came = lax.ppermute(send, "local", other_core)
    keep = pl.pallas_call(
        own_side(groups, members, per_owner),
        out_shape=half,
        scratch_shapes=[pltpu.VMEM((members * per_owner * groups // 2, edges), BF16)],
        compiler_params=params,
        name="own_side",
    )(terms, place, tail)
    chip_sum = (came.astype(F32) + keep.astype(F32)).astype(BF16)
    parts = lax.all_to_all(chip_sum, "local", 0, 0, axis_index_groups=along_x, tiled=True)
    summed = pl.pallas_call(
        member_sum(per_owner, OWNERS),
        out_shape=jax.ShapeDtypeStruct((groups, 2, payload // 2), BF16),
        compiler_params=params,
        name="member_sum",
    )(parts)
    arrived = lax.all_to_all(summed, "group", 0, 0, tiled=True)
    rows = pl.pallas_call(
        grad_rows(per_owner, width),
        out_shape=jax.ShapeDtypeStruct((OWNERS, lines, 128), BF16),
        compiler_params=params,
        name="grad_rows",
    )(arrived)
    rows, base = lax.optimization_barrier((rows, base))
    blocks = [list(range(first, first + OWNERS)) for first in range(0, groups, OWNERS)]
    spread = lax.all_to_all(rows, "group", 0, 0, axis_index_groups=blocks, tiled=True)
    grad_x = pl.pallas_call(
        finish_kernel,
        out_shape=jax.ShapeDtypeStruct((nodes, width), BF16),
        compiler_params=params,
        name="finish",
    )(arrived, recv_rows.reshape(groups, per_owner).T, base)
    spread, grad_x = lax.optimization_barrier((spread, grad_x))
    mine = jnp.broadcast_to(spread[None], (members, OWNERS, lines, 128))
    grads = lax.all_to_all(mine, "local", 0, 0, tiled=True)
    grad_self, grad_neigh = pl.pallas_call(
        widen_kernel,
        out_shape=(jax.ShapeDtypeStruct((width, width), F32), jax.ShapeDtypeStruct((width, width), F32)),
        compiler_params=params,
        name="widen",
    )(grads)
    return (grad_x, grad_self, grad_neigh)


def solution(mesh):
    both = ("group", "local")
    placed = (
        P(both, None),
        P(both, None),
        P(both, None),
        P(both, None),
        P(),
        P(),
        P(both, None, None),
        P(both),
        P(both),
        P(both),
        P(both),
        P(both),
        P("group", None, "local"),
    )
    return jax.shard_map(
        on_device,
        mesh=mesh,
        in_specs=placed,
        out_specs=(P(both, None), P(), P()),
        check_vma=False,
    )
```
